512 devices in a mesh: rows: 16 (over x_lo, z), cols: 32 (over x_hi, y, core).
Axes of the slice: x: 4 (x_hi: 2, x_lo: 2; x = x_hi * 2 + x_lo), y: 8, z: 8, core: 2. Of those that a mesh axis runs over, the one named last changes fastest.
Arguments:
- image_embed: bfloat16 [262144, 1152], P(('rows', 'cols')), may hold values from -0.1875 to 0.1875
- text_embed: bfloat16 [262144, 1152], P(('rows', 'cols')), may hold values from -0.1875 to 0.1875
- pair_ids: int32 [262144], P(('rows', 'cols')), may hold values from 0 to 262143, as said below
- log_scale: float32 [1], replicated, may hold values from 1.6 to 3
- logit_bias: float32 [1], replicated, may hold values from -3 to -1
Outputs:
- row_loss: float32 [262144], P(('rows', 'cols'))
- grad_image: bfloat16 [262144, 1152], P(('rows', 'cols'))
- grad_text: bfloat16 [262144, 1152], P(('rows', 'cols'))
The draws below stay inside these ranges and needn't reach their ends.
Inputs may be any that keep to these rules, and one draw needn't show every extreme that they name: `pair_ids`: positions 0 to 262143 fall in aligned groups of 1024 positions; the id of a pair lies within its own group's range of positions, so pairs of different groups never match.
All inputs are finite; a program needn't handle non-finite values.
Results may differ from the reference program's by a relative error of at most 0.005.
Values may be sent and summed in bfloat16 or wider, within the bound.
No kernel may reach another device: no remote copies, remote signals or barrier semaphores. Data moves between devices by JAX's collectives and lax.ppermute only.
A program may use at most 64 MiB of HBM per device.

```python
import jax
import jax.numpy as jnp
from jax import lax

D = 1152
TOK_DEV = 512
STEPS = 4
TOKENS = 262144


def draw_pair_ids(key, part):
    key = jax.random.fold_in(key, 7)
    group = 2 * TOK_DEV
    position = jnp.arange(TOKENS, dtype=jnp.int32)
    base = position // group * group
    offset = jax.random.randint(key, (TOKENS,), 0, group, dtype=jnp.int32)
    offset = jnp.where(position % group == group - 1, group - 1, offset)
    offset = jnp.where(position % group == 0, 0, offset)
    return (base + offset).astype(jnp.int32)


def shard_levels(own_key, shape, shards, smallest, high):
    level = 1.0
    for axis_at, blocks in shards:
        heights = jax.random.uniform(jax.random.fold_in(jax.random.fold_in(own_key, 6), axis_at), (blocks,), jnp.float32, smallest / len(shards), high / len(shards))
        level = level * jnp.repeat(jnp.exp(heights), shape[axis_at] // blocks).reshape((-1,) + (1,) * (len(shape) - 1 - axis_at))
    return level


def gaussian(own_key, shape, width, most, cuts=(), held_as=jnp.bfloat16):
    values = jax.random.normal(own_key, shape, jnp.float32) * width
    if len(cuts) > 0:
        values = shard_levels(own_key, shape, cuts, -0.22, 0.18) * values
    return jnp.clip(values, min=-most, max=most).astype(held_as)


def setup_inputs(seed: int = 0) -> dict:
    key_of = jax.random.split(jax.random.key(seed), 6)
    image_embed = gaussian(key_of[0], (TOKENS, D), D ** -0.5, 0.1875, ((0, 512),))
    text_embed = gaussian(key_of[1], (TOKENS, D), D ** -0.5, 0.1875, ((0, 512),))
    pair_ids = draw_pair_ids(jax.random.fold_in(key_of[5], 71), 0)
    log_scale = jnp.clip(jax.random.uniform(key_of[3], (1,), jnp.float32, 1.6, 3.0), 1.6, 3.0)
    logit_bias = jnp.clip(jax.random.uniform(key_of[4], (1,), jnp.float32, -3.0, -1.0), -3.0, -1.0)
    return dict(image_embed=image_embed, text_embed=text_embed, pair_ids=pair_ids, log_scale=log_scale, logit_bias=logit_bias)


def block_terms(image_block, text_block, own_ids, other_ids, logit_scale, shift_term):
    logits = logit_scale * jnp.dot(image_block, text_block.T, preferred_element_type=jnp.float32) + shift_term
    positive = (own_ids[:, None] == other_ids[None, :]).astype(jnp.float32)
    row_terms = jnp.sum(jax.nn.softplus(logits) - positive * logits, axis=1)
    slopes = (jax.nn.sigmoid(logits) - positive).astype(jnp.bfloat16)
    image_part = jnp.dot(slopes, text_block, preferred_element_type=jnp.float32)
    text_part = jnp.dot(slopes.T, image_block, preferred_element_type=jnp.float32)
    return row_terms, image_part, text_part


def reference(image_embed, text_embed, pair_ids, log_scale, logit_bias):
    logit_scale = jnp.exp(log_scale[0])
    shift_term = logit_bias[0]
    blocks = TOKENS // TOK_DEV
    images = image_embed.reshape(blocks, TOK_DEV, D)
    texts = text_embed.reshape(blocks, TOK_DEV, D)
    id_blocks = pair_ids.reshape(blocks, TOK_DEV)
    loss_sum = jnp.zeros((blocks, TOK_DEV), jnp.float32)
    image_total = jnp.zeros((blocks, TOK_DEV, D), jnp.float32)
    text_total = jnp.zeros((blocks, TOK_DEV, D), jnp.float32)
    for k in range(STEPS):
        moved_text = jnp.roll(texts, k, axis=0)
        moved_ids = jnp.roll(id_blocks, k, axis=0)

        def one_block(pieces):
            return block_terms(pieces[0], pieces[1], pieces[2], pieces[3], logit_scale, shift_term)

        row_terms, image_part, text_part = lax.map(one_block, (images, moved_text, id_blocks, moved_ids))
        loss_sum = loss_sum + row_terms
        image_total = image_total + image_part
        text_total = text_total + jnp.roll(text_part, -k, axis=0)
    row_loss = (loss_sum / (STEPS * TOK_DEV)).reshape(TOKENS)
    grad_image = (logit_scale * image_total).astype(jnp.bfloat16).reshape(TOKENS, D)
    grad_text = (logit_scale * text_total).astype(jnp.bfloat16).reshape(TOKENS, D)
    return row_loss, grad_image, grad_text
```

```python
import jax
import jax.numpy as jnp
from jax import lax
from jax.sharding import PartitionSpec as P

STEPS = 4
AXES = ("rows", "cols")


def swap_in_chip(size):
    return [(i, i ^ 1) for i in range(size)]


def swap_across(size):
    return [(i, (i + 1) % size if i % 2 else (i - 1) % size) for i in range(size)]


def two_along(size):
    return [(i, (i - 2) % size if i % 2 else (i + 2) % size) for i in range(size)]


def scores(own, other, scale, shift):
    return scale * lax.dot_general(
        own, other, (((1,), (1,)), ((), ())), preferred_element_type=jnp.float32
    ) + shift


def times(slopes, other):
    return jnp.dot(slopes, other, preferred_element_type=jnp.float32)


def far_pair(own, other, scale, shift):
    logits = scores(own, other, scale, shift)
    row_terms = jnp.sum(jax.nn.softplus(logits), axis=1)
    slopes = jax.nn.sigmoid(logits).astype(jnp.bfloat16)
    return row_terms, times(slopes, other)


def near_slopes(own, other, own_ids, other_ids, scale, shift):
    logits = scores(own, other, scale, shift)
    positive = (own_ids[:, None] == other_ids[None, :]).astype(jnp.float32)
    row_terms = jnp.sum(jax.nn.softplus(logits) - positive * logits, axis=1)
    return row_terms, (jax.nn.sigmoid(logits) - positive).astype(jnp.bfloat16)


def after(array, *others):
    return lax.optimization_barrier((array,) + others)[0]


def local(image, text, ids, log_scale, logit_bias):
    scale = jnp.exp(log_scale[0])
    shift = logit_bias[0]
    rows = image.shape[0]
    size = lax.axis_size(AXES)
    even = lax.rem(lax.axis_index(AXES), 2) == 0
    ahead = jnp.where(even, image, text)
    beside = jnp.where(even, text, image)

    cross1 = lax.ppermute(ahead, AXES, swap_across(size))
    chip1 = lax.ppermute(beside, AXES, swap_in_chip(size))
    chip_ids = lax.ppermute(ids, AXES, swap_in_chip(size))

    loss, slopes = near_slopes(image, text, ids, ids, scale, shift)
    image_total = times(slopes, text)
    text_total = times(slopes.T, image)

    cross2 = lax.ppermute(after(beside, image_total, text_total), AXES, two_along(size))

    chip_loss, slopes = near_slopes(beside, chip1, ids, chip_ids, scale, shift)
    chip_total = times(slopes, chip1)

    cross3 = lax.ppermute(cross1, AXES, two_along(size))
    chip2 = lax.ppermute(cross1, AXES, swap_in_chip(size))
    cross_loss, cross_total = far_pair(ahead, cross1, scale, shift)
    more_loss, more = far_pair(beside, chip2, scale, shift)
    chip_loss, chip_total = chip_loss + more_loss, chip_total + more

    chip3 = lax.ppermute(cross2, AXES, swap_in_chip(size))
    more_loss, more = far_pair(ahead, cross2, scale, shift)
    cross_loss, cross_total = cross_loss + more_loss, cross_total + more
    more_loss, more = far_pair(beside, chip3, scale, shift)
    chip_loss, chip_total = chip_loss + more_loss, chip_total + more

    more_loss, more = far_pair(ahead, cross3, scale, shift)
    cross_loss, cross_total = cross_loss + more_loss, cross_total + more

    row_loss = (loss + jnp.where(even, cross_loss, chip_loss)) / (STEPS * rows)
    image_total = image_total + jnp.where(even, cross_total, chip_total)
    text_total = text_total + jnp.where(even, chip_total, cross_total)
    grad_image = (scale * image_total).astype(jnp.bfloat16)
    grad_text = (scale * text_total).astype(jnp.bfloat16)
    return row_loss, grad_image, grad_text


def solution(mesh):
    in_specs = (P(AXES, None), P(AXES, None), P(AXES), P(), P())
    out_specs = (P(AXES), P(AXES, None), P(AXES, None))
    return jax.shard_map(local, mesh=mesh, in_specs=in_specs, out_specs=out_specs, check_vma=False)
```

```python
import functools

import jax
import jax.numpy as jnp
from jax import lax
from jax.experimental import pallas as pl
from jax.experimental.pallas import tpu as pltpu
from jax.sharding import PartitionSpec as P

STEPS = 4
AXES = ("rows", "cols")
LANES = 128
COLUMNS = 256
VMEM_LIMIT = 24 * 1024 * 1024


def swap_in_chip(size):
    return [(i, i ^ 1) for i in range(size)]


def swap_across(size):
    return [(i, (i + 1) % size if i % 2 else (i - 1) % size) for i in range(size)]


def two_along(size):
    return [(i, (i - 2) % size if i % 2 else (i + 2) % size) for i in range(size)]


def after(array, *others):
    return lax.optimization_barrier((array,) + others)[0]


def is_even():
    return lax.rem(lax.axis_index("cols"), 2) == 0


def product(left, right, over_left, over_right):
    return lax.dot_general(
        left, right, (((over_left,), (over_right,)), ((), ())), preferred_element_type=jnp.float32
    )


def scale_of(log_scale_ref):
    return jnp.exp(jnp.full((1, LANES), log_scale_ref[0], jnp.float32))[:, :1]


def fold(terms):
    total = terms[:, :LANES]
    for at in range(LANES, terms.shape[1], LANES):
        total = total + terms[:, at : at + LANES]
    return total


def terms_and_slopes(logits, positive=None):
    small = jnp.exp(-jnp.abs(logits))
    terms = jnp.maximum(logits, 0.0) + jnp.log1p(small)
    slopes = jnp.where(logits >= 0, 1.0, small) / (1.0 + small)
    if positive is not None:
        terms = terms - jnp.where(positive, logits, 0.0)
        slopes = slopes - jnp.where(positive, 1.0, 0.0)
    return terms, slopes.astype(jnp.bfloat16)


def place_kernel(even_ref, odd_ref, out_ref, sem):
    def copy(ref):
        moved = pltpu.make_async_copy(ref, out_ref, sem)
        moved.start()
        moved.wait()

    even = is_even()

    @pl.when(even)
    def _():
        copy(even_ref)

    @pl.when(jnp.logical_not(even))
    def _():
        copy(odd_ref)


def ids_down(ids_ref):
    ids = ids_ref[...]
    return jnp.broadcast_to(ids, (LANES, ids.shape[1])).T


def match(down, ids_ref, columns):
    parts = [
        down == ids_ref[:, at : at + LANES]
        for at in range(columns.start, columns.stop, LANES)
    ]
    return jnp.concatenate(parts, axis=1)


def own_kernel(image_ref, text_ref, ids_ref, log_scale_ref, bias_ref, ahead_ref, beside_ref, loss_ref, slopes_ref):
    scale, shift = scale_of(log_scale_ref), bias_ref[0]
    down = ids_down(ids_ref)
    rows = image_ref.shape[0]
    for at in range(0, rows, COLUMNS):
        columns = slice(at, at + COLUMNS)
        logits = scale * product(image_ref[...], text_ref[columns, :], 1, 1) + shift
        terms, slopes = terms_and_slopes(logits, match(down, ids_ref, columns))
        slopes_ref[:, columns] = slopes
        loss_ref[...] = fold(terms) if at == 0 else loss_ref[...] + fold(terms)

    def parts(image_total, text_total):
        image_total[...] = product(slopes_ref[...], text_ref[...], 1, 0)
        text_total[...] = product(slopes_ref[...], image_ref[...], 0, 0)

    even = is_even()

    @pl.when(even)
    def _():
        parts(ahead_ref, beside_ref)

    @pl.when(jnp.logical_not(even))
    def _():
        parts(beside_ref, ahead_ref)


def pair(own_ref, other_ref, log_scale_ref, bias_ref, total_in, loss_in, total_ref, loss_ref, image_if_even, ids=None):
    scale, shift = scale_of(log_scale_ref), bias_ref[0]
    counted = jnp.where(is_even() == image_if_even, 1.0, 0.0)
    rows = own_ref.shape[0]
    down = None if ids is None else ids_down(ids[0])
    for at in range(0, rows, COLUMNS):
        columns = slice(at, at + COLUMNS)
        logits = scale * product(own_ref[...], other_ref[columns, :], 1, 1) + shift
        positive = None if ids is None else match(down, ids[1], columns)
        terms, slopes = terms_and_slopes(logits, positive)
        first = at == 0
        loss_ref[...] = (loss_in if first else loss_ref)[...] + counted * fold(terms)
        total_ref[...] = (total_in if first else total_ref)[...] + product(slopes, other_ref[columns, :], 1, 0)


def near_kernel(own_ref, other_ref, ids_ref, other_ids_ref, log_scale_ref, bias_ref, total_in, loss_in, total_ref, loss_ref):
    pair(own_ref, other_ref, log_scale_ref, bias_ref, total_in, loss_in, total_ref, loss_ref, False, (ids_ref, other_ids_ref))


def far_kernel(image_if_even, own_ref, other_ref, log_scale_ref, bias_ref, total_in, loss_in, total_ref, loss_ref):
    pair(own_ref, other_ref, log_scale_ref, bias_ref, total_in, loss_in, total_ref, loss_ref, image_if_even)


def write_out(total, log_scale_ref, rounded_ref, sem, first_ref, second_ref):
    rounded_ref[...] = (scale_of(log_scale_ref) * total[...]).astype(jnp.bfloat16)

    def copy(ref):
        moved = pltpu.make_async_copy(rounded_ref, ref, sem)
        moved.start()
        moved.wait()

    even = is_even()

    @pl.when(even)
    def _():
        copy(first_ref)

    @pl.when(jnp.logical_not(even))
    def _():
        copy(second_ref)


def beside_kernel(own_ref, other_ref, log_scale_ref, bias_ref, total_in, loss_in, loss_ref, image_ref, text_ref, total_ref, rounded_ref, sem):
    pair(own_ref, other_ref, log_scale_ref, bias_ref, total_in, loss_in, total_ref, loss_ref, False)
    write_out(total_ref, log_scale_ref, rounded_ref, sem, text_ref, image_ref)


def ahead_kernel(own_ref, other_ref, log_scale_ref, bias_ref, total_in, loss_in, image_in, text_in, row_loss_ref, image_ref, text_ref, total_ref, loss_ref, rounded_ref, sem):
    del image_in, text_in
    pair(own_ref, other_ref, log_scale_ref, bias_ref, total_in, loss_in, total_ref, loss_ref, True)
    rows = own_ref.shape[0]
    row_loss_ref[...] = jnp.sum(loss_ref[...].T, axis=0, keepdims=True) / (STEPS * rows)
    write_out(total_ref, log_scale_ref, rounded_ref, sem, image_ref, text_ref)


def call(kernel, out_shape, in_specs, out_specs, scratch=(), aliases=None, flops=0, moved=0, exps=0):
    return pl.pallas_call(
        kernel,
        out_shape=out_shape,
        in_specs=in_specs,
        out_specs=out_specs,
        scratch_shapes=scratch,
        input_output_aliases=aliases or {},
        cost_estimate=pl.CostEstimate(flops=flops, bytes_accessed=moved, transcendentals=exps),
        compiler_params=pltpu.CompilerParams(vmem_limit_bytes=VMEM_LIMIT),
    )


def near(array):
    return pltpu.with_memory_space_constraint(array, pltpu.VMEM)


def local(image, text, ids, log_scale, logit_bias):
    size = lax.axis_size(AXES)
    rows, width = image.shape
    in_vmem = pl.BlockSpec(memory_space=pltpu.VMEM)
    in_smem = pl.BlockSpec(memory_space=pltpu.SMEM)
    anywhere = pl.BlockSpec(memory_space=pl.ANY)
    total_shape = pltpu.VMEM((rows, width), jnp.float32)
    loss_shape = pltpu.VMEM((rows, LANES), jnp.float32)
    block_shape = pltpu.VMEM((rows, width), jnp.bfloat16)
    grad_shape = jax.ShapeDtypeStruct((rows, width), jnp.bfloat16)
    flops = 2 * rows * rows * width
    costs = dict(flops=2 * flops, exps=3 * rows * rows)

    place = call(place_kernel, block_shape, [anywhere] * 2, in_vmem, [pltpu.SemaphoreType.DMA], moved=2 * rows * width * 2)
    ahead = place(image, text)
    cross1 = lax.ppermute(ahead, AXES, swap_across(size))
    beside = place(text, after(image, ahead))
    chip1 = lax.ppermute(beside, AXES, swap_in_chip(size))
    chip_ids = lax.ppermute(ids, AXES, swap_in_chip(size))

    ids, chip_ids = ids.reshape(1, rows), chip_ids.reshape(1, rows)
    ahead_total, beside_total, loss = call(
        own_kernel,
        (total_shape, total_shape, loss_shape),
        [in_vmem] * 3 + [in_smem] * 2,
        (in_vmem, in_vmem, in_vmem),
        [pltpu.VMEM((rows, rows), jnp.bfloat16)],
        flops=3 * flops,
        exps=3 * rows * rows,
    )(image, text, ids, log_scale, logit_bias)

    chain = dict(aliases={4: 0, 5: 1}, **costs)
    far_specs = [in_vmem] * 2 + [in_smem] * 2 + [in_vmem] * 2

    def far(image_if_even, own, other, total, loss):
        return call(
            functools.partial(far_kernel, image_if_even), (total_shape, loss_shape), far_specs, (in_vmem, in_vmem), **chain
        )(near(own), near(other), log_scale, logit_bias, near(total), near(loss))

    beside_total, loss = call(
        near_kernel,
        (total_shape, loss_shape),
        [in_vmem] * 4 + [in_smem] * 2 + [in_vmem] * 2,
        (in_vmem, in_vmem),
        aliases={6: 0, 7: 1},
        **costs,
    )(near(beside), near(chip1), ids, chip_ids, log_scale, logit_bias, near(beside_total), near(loss))

    cross2 = lax.ppermute(after(beside, loss), AXES, two_along(size))
    cross3 = lax.ppermute(cross1, AXES, two_along(size))
    chip2 = lax.ppermute(cross1, AXES, swap_in_chip(size))
    ahead_total, loss = far(True, ahead, cross1, ahead_total, loss)
    beside_total, loss = far(False, beside, chip2, beside_total, loss)

    chip3 = lax.ppermute(cross2, AXES, swap_in_chip(size))
    ahead_total, loss = far(True, ahead, cross2, ahead_total, loss)
    loss, grad_image, grad_text = call(
        beside_kernel,
        (loss_shape, grad_shape, grad_shape),
        far_specs,
        (in_vmem, anywhere, anywhere),
        [pltpu.VMEM((rows, width), jnp.float32), pltpu.VMEM((rows, width), jnp.bfloat16), pltpu.SemaphoreType.DMA],
        aliases={5: 0},
        **costs,
    )(near(beside), near(chip3), log_scale, logit_bias, near(beside_total), near(loss))

    row_loss, grad_image, grad_text = call(
        ahead_kernel,
        (jax.ShapeDtypeStruct((1, rows), jnp.float32), grad_shape, grad_shape),
        far_specs + [anywhere] * 2,
        (in_vmem, anywhere, anywhere),
        [
            pltpu.VMEM((rows, width), jnp.float32),
            pltpu.VMEM((rows, LANES), jnp.float32),
            pltpu.VMEM((rows, width), jnp.bfloat16),
            pltpu.SemaphoreType.DMA,
        ],
        aliases={6: 1, 7: 2},
        **costs,
    )(near(ahead), near(cross3), log_scale, logit_bias, near(ahead_total), near(loss), grad_image, grad_text)
    return row_loss.reshape(rows), grad_image, grad_text


def solution(mesh):
    in_specs = (P(AXES, None), P(AXES, None), P(AXES), P(), P())
    out_specs = (P(AXES), P(AXES, None), P(AXES, None))
    return jax.shard_map(local, mesh=mesh, in_specs=in_specs, out_specs=out_specs, check_vma=False)
```

```python
import functools

import jax
import jax.numpy as jnp
from jax import lax
from jax.experimental import pallas as pl
from jax.experimental.pallas import tpu as pltpu
from jax.sharding import PartitionSpec as P

STEPS = 4
DIGITS = 3
AXES = ("rows", "cols")
LANES = 128
SPARE = 16
VMEM_LIMIT = 24 * 1024 * 1024


def swap_in_chip(size):
    return [(i, i ^ 1) for i in range(size)]


def swap_across(size):
    return [(i, (i + 1) % size if i % 2 else (i - 1) % size) for i in range(size)]


def two_along(size):
    return [(i, (i - 2) % size if i % 2 else (i + 2) % size) for i in range(size)]


def after(array, *others):
    return lax.optimization_barrier((array,) + others)[0]


def is_even():
    return lax.rem(lax.axis_index("cols"), 2) == 0


def product(left, right, over_left, over_right):
    return lax.dot_general(
        left, right, (((over_left,), (over_right,)), ((), ())), preferred_element_type=jnp.float32
    )


def scale_of(log_scale_ref):
    return jnp.exp(jnp.full((1, LANES), log_scale_ref[0], jnp.float32))[:, :1]


def fold(terms):
    total = terms[:, :LANES]
    for at in range(LANES, terms.shape[1], LANES):
        total = total + terms[:, at : at + LANES]
    return total


def terms_and_slopes(logits, positive=None):
    small = jnp.exp(-jnp.abs(logits))
    terms = jnp.maximum(logits, 0.0) + jnp.log1p(small)
    slopes = jnp.where(logits >= 0, 1.0, small) / (1.0 + small)
    if positive is not None:
        terms = terms - jnp.where(positive, logits, 0.0)
        slopes = slopes - jnp.where(positive, 1.0, 0.0)
    return terms, slopes.astype(jnp.bfloat16)


def copy_by_parity(if_even, if_odd, out, sem):
    even = is_even()
    copies = [(even, pltpu.make_async_copy(if_even, out, sem)), (jnp.logical_not(even), pltpu.make_async_copy(if_odd, out, sem))]
    for here, copy in copies:
        pl.when(here)(copy.start)

    def wait():
        for here, copy in copies:
            pl.when(here)(copy.wait)

    return wait


def ahead_place_kernel(even_ref, odd_ref, out_ref, sem):
    rows, width = even_ref.shape
    wait = copy_by_parity(even_ref, odd_ref, out_ref.at[:rows, :], sem)
    out_ref[rows:, :] = jnp.zeros((SPARE, width), out_ref.dtype)
    wait()


def beside_place_kernel(even_ref, odd_ref, ids_ref, out_ref, with_ids_ref, sems):
    rows, width = even_ref.shape
    waits = [
        copy_by_parity(even_ref, odd_ref, with_ids_ref.at[:rows, :], sems.at[0]),
        copy_by_parity(even_ref, odd_ref, out_ref, sems.at[1]),
    ]
    spare = jnp.zeros((SPARE, width), jnp.float32)
    at_row = lax.broadcasted_iota(jnp.int32, (SPARE, rows), 0)
    ids = jnp.broadcast_to(ids_ref[...], (SPARE, rows))
    digits = jnp.zeros((SPARE, rows), jnp.int32)
    for digit in range(DIGITS):
        digits = jnp.where(at_row == digit, lax.shift_right_logical(ids, 6 * digit) & 63, digits)
    spare = jnp.concatenate([digits.astype(jnp.float32), spare[:, rows:]], axis=1)
    with_ids_ref[rows:, :] = spare.astype(with_ids_ref.dtype)
    for wait in waits:
        wait()


def read_ids(with_ids_ref, rows):
    spare = with_ids_ref[rows:, :][:, :rows].astype(jnp.float32)
    place = lax.broadcasted_iota(jnp.int32, (SPARE, rows), 0)
    weights = jnp.zeros((SPARE, rows), jnp.float32)
    for digit in range(DIGITS):
        weights = jnp.where(place == digit, float(64**digit), weights)
    return jnp.sum(spare * weights, axis=0, keepdims=True).astype(jnp.int32)


def ids_down(ids):
    return jnp.broadcast_to(ids, (LANES, ids.shape[1])).T


def match(down, ids):
    parts = [down == ids[:, at : at + LANES] for at in range(0, ids.shape[1], LANES)]
    return jnp.concatenate(parts, axis=1)


def halves(rows):
    return [slice(0, rows // 2), slice(rows // 2, rows)]


def block_rows(ref, like):
    return ref.at[: like.shape[0], :]


def own_kernel(ahead_ref, beside_ref, ids_ref, log_scale_ref, bias_ref, ahead_total, beside_total, loss_ref, slopes_ref):
    scale, shift = scale_of(log_scale_ref), bias_ref[0]
    ids = ids_ref[...]
    down = ids_down(ids)
    ahead_ref = block_rows(ahead_ref, beside_ref)

    def parts(image_ref, text_ref, image_total, text_total):
        for chunk in halves(image_ref.shape[0]):
            logits = scale * product(image_ref[chunk, :], text_ref[...], 1, 1) + shift
            terms, slopes = terms_and_slopes(logits, match(down[chunk, :], ids))
            loss_ref[chunk, :] = fold(terms)
            slopes_ref[chunk, :] = slopes
            image_total[chunk, :] = product(slopes, text_ref[...], 1, 0)
        text_total[...] = product(slopes_ref[...], image_ref[...], 0, 0)

    even = is_even()

    @pl.when(even)
    def _():
        parts(ahead_ref, beside_ref, ahead_total, beside_total)

    @pl.when(jnp.logical_not(even))
    def _():
        parts(beside_ref, ahead_ref, beside_total, ahead_total)


def pair(own_ref, other_ref, log_scale_ref, bias_ref, total_in, loss_in, loss_ref, image_if_even, store, ids=None):
    scale, shift = scale_of(log_scale_ref), bias_ref[0]
    own_ref, other_ref = block_rows(own_ref, total_in), block_rows(other_ref, total_in)
    counted = jnp.where(is_even() == image_if_even, 1.0, 0.0)
    down = None if ids is None else ids_down(ids[0])
    chunks = halves(own_ref.shape[0])

    def scores(chunk):
        return scale * product(own_ref[chunk, :], other_ref[...], 1, 1) + shift

    logits = scores(chunks[0])
    for at, chunk in enumerate(chunks):
        positive = None if ids is None else match(down[chunk, :], ids[1])
        terms, slopes = terms_and_slopes(logits, positive)
        loss_ref[chunk, :] = loss_in[chunk, :] + counted * fold(terms)
        if at + 1 < len(chunks):
            logits = scores(chunks[at + 1])
        store(chunk, total_in[chunk, :] + product(slopes, other_ref[...], 1, 0))


def keep(total_ref):
    def store(chunk, total):
        total_ref[chunk, :] = total

    return store


def near_kernel(own_ref, other_ref, ids_ref, log_scale_ref, bias_ref, total_in, loss_in, total_ref, loss_ref):
    pair(own_ref, other_ref, log_scale_ref, bias_ref, total_in, loss_in, loss_ref, False, keep(total_ref), (ids_ref[...], read_ids(other_ref, total_in.shape[0])))


def far_kernel(image_if_even, own_ref, other_ref, log_scale_ref, bias_ref, total_in, loss_in, total_ref, loss_ref):
    pair(own_ref, other_ref, log_scale_ref, bias_ref, total_in, loss_in, loss_ref, image_if_even, keep(total_ref))


class Writer:
    def __init__(self, log_scale_ref, rounded_ref, sems, if_even, if_odd):
        self.scale = scale_of(log_scale_ref)
        self.rounded, self.sems, self.outs = rounded_ref, sems, (if_even, if_odd)
        self.chunks = []

    def copies(self, chunk, at):
        even = is_even()
        for out, here in zip(self.outs, (even, jnp.logical_not(even)), strict=True):
            copy = pltpu.make_async_copy(self.rounded.at[chunk, :], out.at[chunk, :], self.sems.at[at])
            yield here, copy

    def __call__(self, chunk, total):
        self.rounded[chunk, :] = (self.scale * total).astype(jnp.bfloat16)
        for here, copy in self.copies(chunk, len(self.chunks)):
            pl.when(here)(copy.start)
        self.chunks.append(chunk)

    def finish(self):
        for at, chunk in enumerate(self.chunks):
            for here, copy in self.copies(chunk, at):
                pl.when(here)(copy.wait)


def beside_kernel(own_ref, other_ref, log_scale_ref, bias_ref, total_in, loss_in, loss_ref, image_ref, text_ref, rounded_ref, sems):
    writer = Writer(log_scale_ref, rounded_ref, sems, text_ref, image_ref)
    pair(own_ref, other_ref, log_scale_ref, bias_ref, total_in, loss_in, loss_ref, False, writer)
    writer.finish()


def ahead_kernel(own_ref, other_ref, log_scale_ref, bias_ref, total_in, loss_in, image_in, text_in, row_loss_ref, image_ref, text_ref, loss_ref, rounded_ref, sems):
    del image_in, text_in
    writer = Writer(log_scale_ref, rounded_ref, sems, image_ref, text_ref)
    pair(own_ref, other_ref, log_scale_ref, bias_ref, total_in, loss_in, loss_ref, True, writer)
    rows = loss_ref.shape[0]
    row_loss_ref[...] = jnp.sum(loss_ref[...].T, axis=0, keepdims=True) / (STEPS * rows)
    writer.finish()


def call(kernel, out_shape, in_specs, out_specs, scratch=(), aliases=None):
    return pl.pallas_call(
        kernel,
        out_shape=out_shape,
        in_specs=in_specs,
        out_specs=out_specs,
        scratch_shapes=scratch,
        input_output_aliases=aliases or {},
        cost_estimate=pl.CostEstimate(flops=1, bytes_accessed=1, transcendentals=0),
        compiler_params=pltpu.CompilerParams(vmem_limit_bytes=VMEM_LIMIT),
    )


def near(array):
    return pltpu.with_memory_space_constraint(array, pltpu.VMEM)


def local(image, text, ids, log_scale, logit_bias):
    size = lax.axis_size(AXES)
    rows, width = image.shape
    in_vmem = pl.BlockSpec(memory_space=pltpu.VMEM)
    in_smem = pl.BlockSpec(memory_space=pltpu.SMEM)
    anywhere = pl.BlockSpec(memory_space=pl.ANY)
    total_shape = pltpu.VMEM((rows, width), jnp.float32)
    loss_shape = pltpu.VMEM((rows, LANES), jnp.float32)
    grad_shape = jax.ShapeDtypeStruct((rows, width), jnp.bfloat16)
    in_hbm = lambda array: pltpu.with_memory_space_constraint(array, pltpu.HBM)
    sems = pltpu.SemaphoreType.DMA((2,))

    ahead = call(
        ahead_place_kernel,
        pltpu.VMEM((rows + SPARE, width), jnp.bfloat16),
        [anywhere] * 2,
        in_vmem,
        [pltpu.SemaphoreType.DMA],
    )(in_hbm(image), in_hbm(text))
    cross1 = lax.ppermute(ahead, AXES, swap_across(size))

    ids = ids.reshape(1, rows)
    beside, with_ids = call(
        beside_place_kernel,
        (pltpu.VMEM((rows, width), jnp.bfloat16), pltpu.VMEM((rows + SPARE, width), jnp.bfloat16)),
        [anywhere] * 2 + [in_vmem],
        (in_vmem, in_vmem),
        [sems],
    )(in_hbm(text), in_hbm(after(image, ahead)), ids)
    chip1 = lax.ppermute(with_ids, AXES, swap_in_chip(size))

    ahead_total, beside_total, loss = call(
        own_kernel,
        (total_shape, total_shape, loss_shape),
        [in_vmem] * 3 + [in_smem] * 2,
        (in_vmem, in_vmem, in_vmem),
        [pltpu.VMEM((rows, rows), jnp.bfloat16)],
    )(near(ahead), near(beside), ids, log_scale, logit_bias)
    cross2 = lax.ppermute(after(beside, loss), AXES, two_along(size))

    far_specs = [in_vmem] * 2 + [in_smem] * 2 + [in_vmem] * 2

    def far(image_if_even, own, other, total, loss):
        return call(
            functools.partial(far_kernel, image_if_even), (total_shape, loss_shape), far_specs, (in_vmem, in_vmem), aliases={4: 0, 5: 1}
        )(near(own), near(other), log_scale, logit_bias, near(total), near(loss))

    beside_total, loss = call(
        near_kernel,
        (total_shape, loss_shape),
        [in_vmem] * 3 + [in_smem] * 2 + [in_vmem] * 2,
        (in_vmem, in_vmem),
        aliases={5: 0, 6: 1},
    )(near(beside), near(chip1), ids, log_scale, logit_bias, near(beside_total), near(loss))

    cross3 = lax.ppermute(cross1, AXES, two_along(size))
    chip2 = lax.ppermute(cross1[:rows], AXES, swap_in_chip(size))
    ahead_total, loss = far(True, ahead, cross1, ahead_total, loss)
    chip3 = lax.ppermute(after(cross2, loss), AXES, swap_in_chip(size))
    beside_total, loss = far(False, beside, chip2, beside_total, loss)
    ahead_total, loss = far(True, ahead, cross2, ahead_total, loss)
    loss, grad_image, grad_text = call(
        beside_kernel,
        (loss_shape, grad_shape, grad_shape),
        far_specs,
        (in_vmem, anywhere, anywhere),
        [pltpu.VMEM((rows, width), jnp.bfloat16), sems],
        aliases={5: 0},
    )(near(beside), near(chip3), log_scale, logit_bias, near(beside_total), near(loss))

    row_loss, grad_image, grad_text = call(
        ahead_kernel,
        (jax.ShapeDtypeStruct((1, rows), jnp.float32), grad_shape, grad_shape),
        far_specs + [anywhere] * 2,
        (in_vmem, anywhere, anywhere),
        [pltpu.VMEM((rows, LANES), jnp.float32), pltpu.VMEM((rows, width), jnp.bfloat16), sems],
        aliases={6: 1, 7: 2},
    )(near(ahead), near(cross3), log_scale, logit_bias, near(ahead_total), near(loss), grad_image, grad_text)
    return row_loss.reshape(rows), grad_image, grad_text


def solution(mesh):
    in_specs = (P(AXES, None), P(AXES, None), P(AXES), P(), P())
    out_specs = (P(AXES), P(AXES, None), P(AXES, None))
    return jax.shard_map(local, mesh=mesh, in_specs=in_specs, out_specs=out_specs, check_vma=False)
```

```python
import functools

import jax
import jax.numpy as jnp
from jax import lax
from jax.experimental import pallas as pl
from jax.experimental.pallas import tpu as pltpu
from jax.sharding import PartitionSpec as P

STEPS = 4
DIGITS = 3
AXES = ("rows", "cols")
LANES = 128
SPARE = 16
VMEM_LIMIT = 24 * 1024 * 1024


def swap_in_chip(size):
    return [(i, i ^ 1) for i in range(size)]


def swap_across(size):
    return [(i, (i + 1) % size if i % 2 else (i - 1) % size) for i in range(size)]


def two_along(size):
    return [(i, (i - 2) % size if i % 2 else (i + 2) % size) for i in range(size)]


def after(array, *others):
    return lax.optimization_barrier((array,) + others)[0]


def is_even():
    return lax.rem(lax.axis_index("cols"), 2) == 0


def product(left, right, over_left, over_right):
    return lax.dot_general(
        left, right, (((over_left,), (over_right,)), ((), ())), preferred_element_type=jnp.float32
    )


def scale_and_shift(scalars_ref):
    return scalars_ref[0:1, 0:1], scalars_ref[1:2, 0:1]


def fold(terms):
    total = terms[:, :LANES]
    for at in range(LANES, terms.shape[1], LANES):
        total = total + terms[:, at : at + LANES]
    return total


def by_parity(true_if_even, body):
    even = is_even()

    @pl.when(even)
    def _():
        body(true_if_even)

    @pl.when(jnp.logical_not(even))
    def _():
        body(not true_if_even)


def slopes_of(logits, small, positive=None):
    slopes = jnp.where(logits >= 0, 1.0, small) / (1.0 + small)
    if positive is not None:
        slopes = slopes - jnp.where(positive, 1.0, 0.0)
    return slopes.astype(jnp.bfloat16)


def terms_of(logits, small, positive=None):
    terms = jnp.maximum(logits, 0.0) + jnp.log1p(small)
    if positive is not None:
        terms = terms - jnp.where(positive, logits, 0.0)
    return terms


def copy_by_parity(if_even, if_odd, out, sem):
    even = is_even()
    copies = [(even, pltpu.make_async_copy(if_even, out, sem)), (jnp.logical_not(even), pltpu.make_async_copy(if_odd, out, sem))]
    for here, copy in copies:
        pl.when(here)(copy.start)

    def wait():
        for here, copy in copies:
            pl.when(here)(copy.wait)

    return wait


def ahead_place_kernel(even_ref, odd_ref, out_ref, sem):
    rows, width = even_ref.shape
    wait = copy_by_parity(even_ref, odd_ref, out_ref.at[:rows, :], sem)
    out_ref[rows:, :] = jnp.zeros((SPARE, width), out_ref.dtype)
    wait()


def beside_place_kernel(even_ref, odd_ref, ids_ref, out_ref, sem):
    rows, width = even_ref.shape
    wait = copy_by_parity(even_ref, odd_ref, out_ref.at[:rows, :], sem)
    spare = jnp.zeros((SPARE, width), jnp.float32)
    at_row = lax.broadcasted_iota(jnp.int32, (SPARE, rows), 0)
    ids = jnp.broadcast_to(ids_ref[...], (SPARE, rows))
    digits = jnp.zeros((SPARE, rows), jnp.int32)
    for digit in range(DIGITS):
        digits = jnp.where(at_row == digit, lax.shift_right_logical(ids, 6 * digit) & 63, digits)
    spare = jnp.concatenate([digits.astype(jnp.float32), spare[:, rows:]], axis=1)
    out_ref[rows:, :] = spare.astype(out_ref.dtype)
    wait()


def read_ids(with_ids_ref, rows):
    spare = with_ids_ref[rows:, :][:, :rows].astype(jnp.float32)
    place = lax.broadcasted_iota(jnp.int32, (SPARE, rows), 0)
    weights = jnp.zeros((SPARE, rows), jnp.float32)
    for digit in range(DIGITS):
        weights = jnp.where(place == digit, float(64**digit), weights)
    return jnp.sum(spare * weights, axis=0, keepdims=True).astype(jnp.int32)


def ids_down(ids):
    return jnp.broadcast_to(ids, (LANES, ids.shape[1])).T


def match(down, ids):
    parts = [down == ids[:, at : at + LANES] for at in range(0, ids.shape[1], LANES)]
    return jnp.concatenate(parts, axis=1)


def halves(rows):
    return [slice(0, rows // 2), slice(rows // 2, rows)]


def block_rows(ref, like):
    return ref.at[: like.shape[0], :]


def own_kernel(ahead_ref, with_ids_ref, ids_ref, scalars_ref, beside_ref, slopes_ref, loss_ref, sem):
    beside_copy = pltpu.make_async_copy(block_rows(with_ids_ref, beside_ref), beside_ref, sem)
    beside_copy.start()
    scale, shift = scale_and_shift(scalars_ref)
    ids = ids_ref[...]
    down = ids_down(ids)
    ahead_ref, with_ids_ref = block_rows(ahead_ref, beside_ref), block_rows(with_ids_ref, beside_ref)

    def body(even):
        image_ref, text_ref = (ahead_ref, with_ids_ref) if even else (with_ids_ref, ahead_ref)
        for chunk in halves(image_ref.shape[0]):
            logits = scale * product(image_ref[chunk, :], text_ref[...], 1, 1) + shift
            small, positive = jnp.exp(-jnp.abs(logits)), match(down[chunk, :], ids)
            slopes_ref[chunk, :] = slopes_of(logits, small, positive)
            loss_ref[chunk, :] = fold(terms_of(logits, small, positive))

    by_parity(True, body)
    beside_copy.wait()


def pair(own_ref, other_ref, scalars_ref, total_in, loss_in, loss_ref, image_if_even, store, ids=None):
    scale, shift = scale_and_shift(scalars_ref)
    own_ref, other_ref = block_rows(own_ref, total_in), block_rows(other_ref, total_in)
    down = None if ids is None else ids_down(ids[0])
    chunks = halves(own_ref.shape[0])

    def scores(chunk):
        return scale * product(own_ref[chunk, :], other_ref[...], 1, 1) + shift

    def body(counted):
        logits = scores(chunks[0])
        for at, chunk in enumerate(chunks):
            positive = None if ids is None else match(down[chunk, :], ids[1])
            small = jnp.exp(-jnp.abs(logits))
            slopes = slopes_of(logits, small, positive)
            if counted:
                loss_ref[chunk, :] = loss_in[chunk, :] + fold(terms_of(logits, small, positive))
            else:
                loss_ref[chunk, :] = loss_in[chunk, :]
            if at + 1 < len(chunks):
                logits = scores(chunks[at + 1])
            store(chunk, total_in[chunk, :] + product(slopes, other_ref[...], 1, 0))

    by_parity(image_if_even, body)


def keep(total_ref):
    def store(chunk, total):
        total_ref[chunk, :] = total

    return store


def near_kernel(ahead_ref, own_ref, other_ref, own_slopes_ref, ids_ref, scalars_ref, loss_in, ahead_total, total_ref, loss_ref):
    ahead_ref = block_rows(ahead_ref, own_ref)

    def body(even):
        image_ref, text_ref = (ahead_ref, own_ref) if even else (own_ref, ahead_ref)
        image_total, text_total = (ahead_total, total_ref) if even else (total_ref, ahead_total)
        image_total[...] = product(own_slopes_ref[...], text_ref[...], 1, 0)
        text_total[...] = product(own_slopes_ref[...], image_ref[...], 0, 0)

    by_parity(True, body)
    ids = (ids_ref[...], read_ids(other_ref, own_ref.shape[0]))
    pair(own_ref, other_ref, scalars_ref, total_ref, loss_in, loss_ref, False, keep(total_ref), ids)


def far_kernel(image_if_even, own_ref, other_ref, scalars_ref, total_in, loss_in, total_ref, loss_ref):
    pair(own_ref, other_ref, scalars_ref, total_in, loss_in, loss_ref, image_if_even, keep(total_ref))


def beside_kernel(own_ref, other_ref, scalars_ref, total_in, loss_in, rounded_ref, loss_ref):
    scale, _ = scale_and_shift(scalars_ref)

    def store(chunk, total):
        rounded_ref[chunk, :] = (scale * total).astype(jnp.bfloat16)

    pair(own_ref, other_ref, scalars_ref, total_in, loss_in, loss_ref, False, store)


def ahead_kernel(own_ref, other_ref, scalars_ref, total_in, loss_in, beside_ref, row_loss_ref, image_ref, text_ref, rounded_ref, sems):
    scale, shift = scale_and_shift(scalars_ref)
    own_ref, other_ref = block_rows(own_ref, total_in), block_rows(other_ref, total_in)
    rows = total_in.shape[0]
    chunks = halves(rows)

    def scores(chunk):
        return scale * product(own_ref[chunk, :], other_ref[...], 1, 1) + shift

    def body(even):
        ahead_out, beside_out = (image_ref, text_ref) if even else (text_ref, image_ref)
        copies = [pltpu.make_async_copy(beside_ref, beside_out, sems.at[0])]
        copies[0].start()
        logits = [scores(chunks[0])]
        small = []
        for at, chunk in enumerate(chunks):
            small.append(jnp.exp(-jnp.abs(logits[at])))
            slopes = slopes_of(logits[at], small[at])
            if at + 1 < len(chunks):
                logits.append(scores(chunks[at + 1]))
            total = total_in[chunk, :] + product(slopes, other_ref[...], 1, 0)
            rounded_ref[chunk, :] = (scale * total).astype(jnp.bfloat16)
            copies.append(pltpu.make_async_copy(rounded_ref.at[chunk, :], ahead_out.at[chunk, :], sems.at[at + 1]))
            copies[-1].start()
        for at, chunk in enumerate(chunks):
            loss = loss_in[chunk, :]
            if even:
                loss = loss + fold(terms_of(logits[at], small[at]))
            row_loss_ref[:, chunk] = jnp.sum(loss.T, axis=0, keepdims=True) / (STEPS * rows)
        for copy in copies:
            copy.wait()

    by_parity(True, body)


def call(kernel, out_shape, in_specs, out_specs, scratch=(), aliases=None):
    return pl.pallas_call(
        kernel,
        out_shape=out_shape,
        in_specs=in_specs,
        out_specs=out_specs,
        scratch_shapes=scratch,
        input_output_aliases=aliases or {},
        cost_estimate=pl.CostEstimate(flops=1, bytes_accessed=1, transcendentals=0),
        compiler_params=pltpu.CompilerParams(vmem_limit_bytes=VMEM_LIMIT),
    )


def near(array):
    return pltpu.with_memory_space_constraint(array, pltpu.VMEM)


def local(image, text, ids, log_scale, logit_bias):
    size = lax.axis_size(AXES)
    rows, width = image.shape
    in_vmem = pl.BlockSpec(memory_space=pltpu.VMEM)
    anywhere = pl.BlockSpec(memory_space=pl.ANY)
    total_shape = pltpu.VMEM((rows, width), jnp.float32)
    loss_shape = pltpu.VMEM((rows, LANES), jnp.float32)
    block_shape = pltpu.VMEM((rows, width), jnp.bfloat16)
    grad_shape = jax.ShapeDtypeStruct((rows, width), jnp.bfloat16)
    in_hbm = lambda array: pltpu.with_memory_space_constraint(array, pltpu.HBM)

    ahead = call(
        ahead_place_kernel,
        pltpu.VMEM((rows + SPARE, width), jnp.bfloat16),
        [anywhere] * 2,
        in_vmem,
        [pltpu.SemaphoreType.DMA],
    )(in_hbm(image), in_hbm(text))
    cross1 = lax.ppermute(ahead, AXES, swap_across(size))

    ids = ids.reshape(1, rows)
    with_ids = call(
        beside_place_kernel,
        pltpu.VMEM((rows + SPARE, width), jnp.bfloat16),
        [anywhere] * 2 + [in_vmem],
        in_vmem,
        [pltpu.SemaphoreType.DMA],
    )(in_hbm(text), in_hbm(after(image, ahead)), ids)
    scalars = jnp.where(lax.broadcasted_iota(jnp.int32, (8, LANES), 0) == 0, jnp.exp(log_scale), logit_bias)
    chip1 = lax.ppermute(with_ids, AXES, swap_in_chip(size))

    beside, own_slopes, loss = call(
        own_kernel,
        (block_shape, pltpu.VMEM((rows, rows), jnp.bfloat16), loss_shape),
        [in_vmem] * 4,
        (in_vmem,) * 3,
        [pltpu.SemaphoreType.DMA],
    )(near(ahead), near(with_ids), ids, scalars)
    cross2 = lax.ppermute(beside, AXES, two_along(size))

    far_specs = [in_vmem] * 5

    def far(image_if_even, own, other, total, loss):
        return call(
            functools.partial(far_kernel, image_if_even), (total_shape, loss_shape), far_specs, (in_vmem, in_vmem), aliases={3: 0, 4: 1}
        )(near(own), near(other), scalars, near(total), near(loss))

    ahead_total, beside_total, loss = call(
        near_kernel,
        (total_shape, total_shape, loss_shape),
        [in_vmem] * 7,
        (in_vmem,) * 3,
        aliases={6: 2},
    )(near(ahead), near(beside), near(chip1), near(own_slopes), ids, scalars, near(loss))

    cross1 = after(cross1, loss)
    cross3 = lax.ppermute(cross1, AXES, two_along(size))
    chip2 = lax.ppermute(cross1[:rows], AXES, swap_in_chip(size))
    ahead_total, loss = far(True, ahead, cross1, ahead_total, loss)
    chip3 = lax.ppermute(after(cross2, loss), AXES, swap_in_chip(size))
    beside_total, loss = far(False, beside, chip2, beside_total, loss)
    ahead_total, loss = far(True, ahead, cross2, ahead_total, loss)
    beside_grad, loss = call(
        beside_kernel,
        (block_shape, loss_shape),
        far_specs,
        (in_vmem, in_vmem),
        aliases={4: 1},
    )(near(beside), near(chip3), scalars, near(beside_total), near(loss))

    row_loss, grad_image, grad_text = call(
        ahead_kernel,
        (jax.ShapeDtypeStruct((1, rows), jnp.float32), grad_shape, grad_shape),
        far_specs + [in_vmem],
        (in_vmem, anywhere, anywhere),
        [pltpu.VMEM((rows, width), jnp.bfloat16), pltpu.SemaphoreType.DMA((3,))],
    )(near(ahead), near(cross3), scalars, near(ahead_total), near(loss), near(beside_grad))
    return row_loss.reshape(rows), grad_image, grad_text


def solution(mesh):
    in_specs = (P(AXES, None), P(AXES, None), P(AXES), P(), P())
    out_specs = (P(AXES), P(AXES, None), P(AXES, None))
    return jax.shard_map(local, mesh=mesh, in_specs=in_specs, out_specs=out_specs, check_vma=False)
```

```python
import functools

import jax
import jax.numpy as jnp
from jax import lax
from jax.experimental import pallas as pl
from jax.experimental.pallas import tpu as pltpu
from jax.sharding import PartitionSpec as P

STEPS = 4
DIGITS = 3
AXES = ("rows", "cols")
LANES = 128
SPARE = 16
VMEM_LIMIT = 24 * 1024 * 1024


def swap_in_chip(size):
    return [(i, i ^ 1) for i in range(size)]


def swap_across(size):
    return [(i, (i + 1) % size if i % 2 else (i - 1) % size) for i in range(size)]


def two_along(size):
    return [(i, (i - 2) % size if i % 2 else (i + 2) % size) for i in range(size)]


def after(array, *others):
    return lax.optimization_barrier((array,) + others)[0]


def is_even():
    return lax.rem(lax.axis_index("cols"), 2) == 0


def product(left, right, over_left, over_right):
    return lax.dot_general(
        left, right, (((over_left,), (over_right,)), ((), ())), preferred_element_type=jnp.float32
    )


def scale_and_shift(scalars_ref):
    return scalars_ref[0:1, 0:1], scalars_ref[1:2, 0:1]


def fold(terms):
    total = terms[:, :LANES]
    for at in range(LANES, terms.shape[1], LANES):
        total = total + terms[:, at : at + LANES]
    return total


def by_parity(true_if_even, body):
    even = is_even()

    @pl.when(even)
    def _():
        body(true_if_even)

    @pl.when(jnp.logical_not(even))
    def _():
        body(not true_if_even)


def slopes_of(logits, small, positive=None):
    slopes = jnp.where(logits >= 0, 1.0, small) / (1.0 + small)
    if positive is not None:
        slopes = slopes - jnp.where(positive, 1.0, 0.0)
    return slopes.astype(jnp.bfloat16)


def terms_of(logits, small, positive=None):
    terms = jnp.maximum(logits, 0.0) + jnp.log1p(small)
    if positive is not None:
        terms = terms - jnp.where(positive, logits, 0.0)
    return terms


def copy_by_parity(if_even, if_odd, out, sem):
    even = is_even()
    copies = [(even, pltpu.make_async_copy(if_even, out, sem)), (jnp.logical_not(even), pltpu.make_async_copy(if_odd, out, sem))]
    for here, copy in copies:
        pl.when(here)(copy.start)

    def wait():
        for here, copy in copies:
            pl.when(here)(copy.wait)

    return wait


def ahead_place_kernel(even_ref, odd_ref, out_ref, sem):
    rows, width = even_ref.shape
    wait = copy_by_parity(even_ref, odd_ref, out_ref.at[:rows, :], sem)
    out_ref[rows:, :] = jnp.zeros((SPARE, width), out_ref.dtype)
    wait()


def beside_place_kernel(even_ref, odd_ref, ids_ref, out_ref, sem):
    rows, width = even_ref.shape
    wait = copy_by_parity(even_ref, odd_ref, out_ref.at[:rows, :], sem)
    spare = jnp.zeros((SPARE, width), jnp.float32)
    at_row = lax.broadcasted_iota(jnp.int32, (SPARE, rows), 0)
    ids = jnp.broadcast_to(ids_ref[...], (SPARE, rows))
    digits = jnp.zeros((SPARE, rows), jnp.int32)
    for digit in range(DIGITS):
        digits = jnp.where(at_row == digit, lax.shift_right_logical(ids, 6 * digit) & 63, digits)
    spare = jnp.concatenate([digits.astype(jnp.float32), spare[:, rows:]], axis=1)
    out_ref[rows:, :] = spare.astype(out_ref.dtype)
    wait()


def read_ids(with_ids_ref, rows):
    spare = with_ids_ref[rows:, :][:, :rows].astype(jnp.float32)
    place = lax.broadcasted_iota(jnp.int32, (SPARE, rows), 0)
    weights = jnp.zeros((SPARE, rows), jnp.float32)
    for digit in range(DIGITS):
        weights = jnp.where(place == digit, float(64**digit), weights)
    return jnp.sum(spare * weights, axis=0, keepdims=True).astype(jnp.int32)


def ids_down(ids):
    return jnp.broadcast_to(ids, (LANES, ids.shape[1])).T


def match(down, ids):
    parts = [down == ids[:, at : at + LANES] for at in range(0, ids.shape[1], LANES)]
    return jnp.concatenate(parts, axis=1)


def halves(rows):
    return [slice(0, rows // 2), slice(rows // 2, rows)]


def block_rows(ref, like):
    return ref.at[: like.shape[0], :]


def own_kernel(ahead_ref, with_ids_ref, ids_ref, scalars_ref, beside_ref, slopes_ref, loss_ref, sem):
    beside_copy = pltpu.make_async_copy(block_rows(with_ids_ref, beside_ref), beside_ref, sem)
    beside_copy.start()
    scale, shift = scale_and_shift(scalars_ref)
    ids = ids_ref[...]
    down = ids_down(ids)
    ahead_ref, with_ids_ref = block_rows(ahead_ref, beside_ref), block_rows(with_ids_ref, beside_ref)

    def body(even):
        image_ref, text_ref = (ahead_ref, with_ids_ref) if even else (with_ids_ref, ahead_ref)
        for chunk in halves(image_ref.shape[0]):
            logits = scale * product(image_ref[chunk, :], text_ref[...], 1, 1) + shift
            small, positive = jnp.exp(-jnp.abs(logits)), match(down[chunk, :], ids)
            slopes_ref[chunk, :] = slopes_of(logits, small, positive)
            loss_ref[chunk, :] = fold(terms_of(logits, small, positive))

    by_parity(True, body)
    beside_copy.wait()


def pair(own_ref, other_ref, scalars_ref, total_in, loss_in, loss_ref, image_if_even, store, ids=None):
    scale, shift = scale_and_shift(scalars_ref)
    own_ref, other_ref = block_rows(own_ref, total_in), block_rows(other_ref, total_in)
    down = None if ids is None else ids_down(ids[0])
    chunks = halves(own_ref.shape[0])

    def scores(chunk):
        return scale * product(own_ref[chunk, :], other_ref[...], 1, 1) + shift

    def body(counted):
        logits = scores(chunks[0])
        for at, chunk in enumerate(chunks):
            positive = None if ids is None else match(down[chunk, :], ids[1])
            small = jnp.exp(-jnp.abs(logits))
            slopes = slopes_of(logits, small, positive)
            if counted:
                loss_ref[chunk, :] = loss_in[chunk, :] + fold(terms_of(logits, small, positive))
            else:
                loss_ref[chunk, :] = loss_in[chunk, :]
            if at + 1 < len(chunks):
                logits = scores(chunks[at + 1])
            store(chunk, total_in[chunk, :] + product(slopes, other_ref[...], 1, 0))

    by_parity(image_if_even, body)


def keep(total_ref):
    def store(chunk, total):
        total_ref[chunk, :] = total

    return store


def near_kernel(ahead_ref, own_ref, other_ref, own_slopes_ref, ids_ref, scalars_ref, loss_in, ahead_total, total_ref, loss_ref):
    ahead_ref = block_rows(ahead_ref, own_ref)

    def body(even):
        image_ref, text_ref = (ahead_ref, own_ref) if even else (own_ref, ahead_ref)
        image_total, text_total = (ahead_total, total_ref) if even else (total_ref, ahead_total)
        image_total[...] = product(own_slopes_ref[...], text_ref[...], 1, 0)
        text_total[...] = product(own_slopes_ref[...], image_ref[...], 0, 0)

    by_parity(True, body)
    ids = (ids_ref[...], read_ids(other_ref, own_ref.shape[0]))
    pair(own_ref, other_ref, scalars_ref, total_ref, loss_in, loss_ref, False, keep(total_ref), ids)


def far_kernel(image_if_even, own_ref, other_ref, scalars_ref, total_in, loss_in, total_ref, loss_ref):
    pair(own_ref, other_ref, scalars_ref, total_in, loss_in, loss_ref, image_if_even, keep(total_ref))


def beside_kernel(own_ref, other_ref, scalars_ref, total_in, loss_in, rounded_ref, loss_ref):
    scale, _ = scale_and_shift(scalars_ref)

    def store(chunk, total):
        rounded_ref[chunk, :] = (scale * total).astype(jnp.bfloat16)

    pair(own_ref, other_ref, scalars_ref, total_in, loss_in, loss_ref, False, store)


def ahead_kernel(own_ref, other_ref, scalars_ref, total_in, loss_in, beside_ref, row_loss_ref, image_ref, text_ref, rounded_ref, losses_ref, sems):
    scale, shift = scale_and_shift(scalars_ref)
    own_ref, other_ref = block_rows(own_ref, total_in), block_rows(other_ref, total_in)
    rows = total_in.shape[0]
    chunks = halves(rows)

    def scores(chunk):
        return scale * product(own_ref[chunk, :], other_ref[...], 1, 1) + shift

    def body(even):
        ahead_out, beside_out = (image_ref, text_ref) if even else (text_ref, image_ref)
        copies = [pltpu.make_async_copy(beside_ref, beside_out, sems.at[0])]
        copies[0].start()
        logits = scores(chunks[0])
        for at, chunk in enumerate(chunks):
            last = at + 1 == len(chunks)
            small = jnp.exp(-jnp.abs(logits))
            slopes = slopes_of(logits, small)
            loss = loss_in[chunk, :]
            if even:
                loss = loss + fold(terms_of(logits, small))
            losses_ref[:, chunk] = jnp.sum(loss.T, axis=0, keepdims=True) / (STEPS * rows)
            if last:
                copies.append(pltpu.make_async_copy(losses_ref, row_loss_ref, sems.at[at + 2]))
                copies[-1].start()
            else:
                logits = scores(chunks[at + 1])
            total = total_in[chunk, :] + product(slopes, other_ref[...], 1, 0)
            rounded_ref[chunk, :] = (scale * total).astype(jnp.bfloat16)
            copies.append(pltpu.make_async_copy(rounded_ref.at[chunk, :], ahead_out.at[chunk, :], sems.at[at + 1]))
            copies[-1].start()
        for copy in copies:
            copy.wait()

    by_parity(True, body)


def call(kernel, out_shape, in_specs, out_specs, scratch=(), aliases=None):
    return pl.pallas_call(
        kernel,
        out_shape=out_shape,
        in_specs=in_specs,
        out_specs=out_specs,
        scratch_shapes=scratch,
        input_output_aliases=aliases or {},
        cost_estimate=pl.CostEstimate(flops=1, bytes_accessed=1, transcendentals=0),
        compiler_params=pltpu.CompilerParams(vmem_limit_bytes=VMEM_LIMIT),
    )


def near(array):
    return pltpu.with_memory_space_constraint(array, pltpu.VMEM)


def local(image, text, ids, log_scale, logit_bias):
    size = lax.axis_size(AXES)
    rows, width = image.shape
    in_vmem = pl.BlockSpec(memory_space=pltpu.VMEM)
    anywhere = pl.BlockSpec(memory_space=pl.ANY)
    total_shape = pltpu.VMEM((rows, width), jnp.float32)
    loss_shape = pltpu.VMEM((rows, LANES), jnp.float32)
    block_shape = pltpu.VMEM((rows, width), jnp.bfloat16)
    grad_shape = jax.ShapeDtypeStruct((rows, width), jnp.bfloat16)
    in_hbm = lambda array: pltpu.with_memory_space_constraint(array, pltpu.HBM)

    ahead = call(
        ahead_place_kernel,
        pltpu.VMEM((rows + SPARE, width), jnp.bfloat16),
        [anywhere] * 2,
        in_vmem,
        [pltpu.SemaphoreType.DMA],
    )(in_hbm(image), in_hbm(text))
    cross1 = lax.ppermute(ahead, AXES, swap_across(size))

    ids = ids.reshape(1, rows)
    with_ids = call(
        beside_place_kernel,
        pltpu.VMEM((rows + SPARE, width), jnp.bfloat16),
        [anywhere] * 2 + [in_vmem],
        in_vmem,
        [pltpu.SemaphoreType.DMA],
    )(in_hbm(text), in_hbm(after(image, ahead)), ids)
    scalars = jnp.where(lax.broadcasted_iota(jnp.int32, (8, LANES), 0) == 0, jnp.exp(log_scale), logit_bias)
    chip1 = lax.ppermute(with_ids, AXES, swap_in_chip(size))

    beside, own_slopes, loss = call(
        own_kernel,
        (block_shape, pltpu.VMEM((rows, rows), jnp.bfloat16), loss_shape),
        [in_vmem] * 4,
        (in_vmem,) * 3,
        [pltpu.SemaphoreType.DMA],
    )(near(ahead), near(with_ids), ids, scalars)
    cross2 = lax.ppermute(beside, AXES, two_along(size))

    far_specs = [in_vmem] * 5

    def far(image_if_even, own, other, total, loss):
        return call(
            functools.partial(far_kernel, image_if_even), (total_shape, loss_shape), far_specs, (in_vmem, in_vmem), aliases={3: 0, 4: 1}
        )(near(own), near(other), scalars, near(total), near(loss))

    ahead_total, beside_total, loss = call(
        near_kernel,
        (total_shape, total_shape, loss_shape),
        [in_vmem] * 7,
        (in_vmem,) * 3,
        aliases={6: 2},
    )(near(ahead), near(beside), near(chip1), near(own_slopes), ids, scalars, near(loss))

    cross1 = after(cross1, loss)
    cross3 = lax.ppermute(cross1, AXES, two_along(size))
    chip2 = lax.ppermute(cross1[:rows], AXES, swap_in_chip(size))
    ahead_total, loss = far(True, ahead, cross1, ahead_total, loss)
    chip3 = lax.ppermute(after(cross2, loss), AXES, swap_in_chip(size))
    beside_total, loss = far(False, beside, chip2, beside_total, loss)
    ahead_total, loss = far(True, ahead, cross2, ahead_total, loss)
    beside_grad, loss = call(
        beside_kernel,
        (block_shape, loss_shape),
        far_specs,
        (in_vmem, in_vmem),
        aliases={4: 1},
    )(near(beside), near(chip3), scalars, near(beside_total), near(loss))

    row_loss, grad_image, grad_text = call(
        ahead_kernel,
        (jax.ShapeDtypeStruct((1, rows), jnp.float32), grad_shape, grad_shape),
        far_specs + [in_vmem],
        (anywhere, anywhere, anywhere),
        [pltpu.VMEM((rows, width), jnp.bfloat16), pltpu.VMEM((1, rows), jnp.float32), pltpu.SemaphoreType.DMA((4,))],
    )(near(ahead), near(cross3), scalars, near(ahead_total), near(loss), near(beside_grad))
    return row_loss.reshape(rows), grad_image, grad_text


def solution(mesh):
    in_specs = (P(AXES, None), P(AXES, None), P(AXES), P(), P())
    out_specs = (P(AXES), P(AXES, None), P(AXES, None))
    return jax.shard_map(local, mesh=mesh, in_specs=in_specs, out_specs=out_specs, check_vma=False)
```

```python
import functools

import jax
import jax.numpy as jnp
from jax import lax
from jax.experimental import pallas as pl
from jax.experimental.pallas import tpu as pltpu
from jax.sharding import PartitionSpec as P

STEPS = 4
DIGITS = 3
AXES = ("rows", "cols")
LANES = 128
RUN = 16
SPARE = 16
VMEM_LIMIT = 24 * 1024 * 1024


def swap_in_chip(size):
    return [(i, i ^ 1) for i in range(size)]


def swap_across(size):
    return [(i, (i + 1) % size if i % 2 else (i - 1) % size) for i in range(size)]


def two_along(size):
    return [(i, (i - 2) % size if i % 2 else (i + 2) % size) for i in range(size)]


def after(array, *others):
    return lax.optimization_barrier((array,) + others)[0]


def is_even():
    return lax.rem(lax.axis_index("cols"), 2) == 0


def product(left, right, over_left, over_right):
    return lax.dot_general(
        left, right, (((over_left,), (over_right,)), ((), ())), preferred_element_type=jnp.float32
    )


def scale_and_shift(scalars_ref):
    return scalars_ref[0:1, 0:1], scalars_ref[1:2, 0:1]


def fold(terms):
    total = terms[:, :LANES]
    for at in range(LANES, terms.shape[1], LANES):
        total = total + terms[:, at : at + LANES]
    return total


def by_parity(true_if_even, body):
    even = is_even()

    @pl.when(even)
    def _():
        body(true_if_even)

    @pl.when(jnp.logical_not(even))
    def _():
        body(not true_if_even)


def slopes_of(logits, small, positive=None):
    slopes = jnp.where(logits >= 0, 1.0, small) / (1.0 + small)
    if positive is not None:
        slopes = slopes - jnp.where(positive, 1.0, 0.0)
    return slopes.astype(jnp.bfloat16)


def terms_of(logits, small, positive=None):
    terms = jnp.maximum(logits, 0.0) + jnp.log1p(small)
    if positive is not None:
        terms = terms - jnp.where(positive, logits, 0.0)
    return terms


def copy_by_parity(if_even, if_odd, out, sem):
    even = is_even()
    copies = [(even, pltpu.make_async_copy(if_even, out, sem)), (jnp.logical_not(even), pltpu.make_async_copy(if_odd, out, sem))]
    for here, copy in copies:
        pl.when(here)(copy.start)

    def wait():
        for here, copy in copies:
            pl.when(here)(copy.wait)

    return wait


def ahead_place_kernel(even_ref, odd_ref, out_ref, sem):
    rows, width = even_ref.shape
    wait = copy_by_parity(even_ref, odd_ref, out_ref.at[:rows, :], sem)
    out_ref[rows:, :] = jnp.zeros((SPARE, width), out_ref.dtype)
    wait()


def beside_place_kernel(even_ref, odd_ref, ids_ref, out_ref, sem):
    rows, width = even_ref.shape
    wait = copy_by_parity(even_ref, odd_ref, out_ref.at[:rows, :], sem)
    spare = jnp.zeros((SPARE, width), jnp.float32)
    at_row = lax.broadcasted_iota(jnp.int32, (SPARE, rows), 0)
    ids = jnp.broadcast_to(ids_ref[...], (SPARE, rows))
    digits = jnp.zeros((SPARE, rows), jnp.int32)
    for digit in range(DIGITS):
        digits = jnp.where(at_row == digit, lax.shift_right_logical(ids, 6 * digit) & 63, digits)
    spare = jnp.concatenate([digits.astype(jnp.float32), spare[:, rows:]], axis=1)
    out_ref[rows:, :] = spare.astype(out_ref.dtype)
    wait()


def read_ids(with_ids_ref, rows):
    spare = with_ids_ref[rows:, :][:, :rows].astype(jnp.float32)
    place = lax.broadcasted_iota(jnp.int32, (SPARE, rows), 0)
    weights = jnp.zeros((SPARE, rows), jnp.float32)
    for digit in range(DIGITS):
        weights = jnp.where(place == digit, float(64**digit), weights)
    return jnp.sum(spare * weights, axis=0, keepdims=True).astype(jnp.int32)


def ids_down(ids):
    return jnp.broadcast_to(ids, (LANES, ids.shape[1])).T


def match(down, ids):
    parts = [down == ids[:, at : at + LANES] for at in range(0, ids.shape[1], LANES)]
    return jnp.concatenate(parts, axis=1)


def halves(rows):
    return [slice(0, rows // 2), slice(rows // 2, rows)]


def block_rows(ref, like):
    return ref.at[: like.shape[0], :]


def on_some(where, body):
    if where is None:
        body()
        return
    places, among = where
    at = lax.rem(lax.axis_index("cols"), RUN)
    here = functools.reduce(jnp.logical_or, [at == place for place in places])
    pl.when(here if among else jnp.logical_not(here))(body)


def own_scores(where, ahead_ref, beside_ref, ids_ref, scalars_ref, slopes_ref, loss_ref):
    def body(even):
        scale, shift = scale_and_shift(scalars_ref)
        ids = ids_ref[...]
        down = ids_down(ids)
        image_ref, text_ref = (ahead_ref, beside_ref) if even else (beside_ref, ahead_ref)
        for chunk in halves(image_ref.shape[0]):
            logits = scale * product(image_ref[chunk, :], text_ref[...], 1, 1) + shift
            small, positive = jnp.exp(-jnp.abs(logits)), match(down[chunk, :], ids)
            slopes_ref[chunk, :] = slopes_of(logits, small, positive)
            loss_ref[chunk, :] = fold(terms_of(logits, small, positive))

    on_some(where, lambda: by_parity(True, body))


def own_products(where, ahead_ref, beside_ref, slopes_ref, ahead_total, beside_total):
    def body(even):
        image_ref, text_ref = (ahead_ref, beside_ref) if even else (beside_ref, ahead_ref)
        image_total, text_total = (ahead_total, beside_total) if even else (beside_total, ahead_total)
        image_total[...] = product(slopes_ref[...], text_ref[...], 1, 0)
        text_total[...] = product(slopes_ref[...], image_ref[...], 0, 0)

    on_some(where, lambda: by_parity(True, body))


def own_kernel(ahead_ref, with_ids_ref, ids_ref, scalars_ref, beside_ref, slopes_ref, loss_ref, sem):
    beside_copy = pltpu.make_async_copy(block_rows(with_ids_ref, beside_ref), beside_ref, sem)
    beside_copy.start()
    ahead_ref, with_ids_ref = block_rows(ahead_ref, beside_ref), block_rows(with_ids_ref, beside_ref)
    own_scores(((0,), False), ahead_ref, with_ids_ref, ids_ref, scalars_ref, slopes_ref, loss_ref)
    beside_copy.wait()


def later_scores_kernel(ahead_ref, beside_ref, ids_ref, scalars_ref, slopes_in, loss_in, slopes_ref, loss_ref):
    own_scores(((0,), True), block_rows(ahead_ref, beside_ref), beside_ref, ids_ref, scalars_ref, slopes_ref, loss_ref)


def early_products_kernel(ahead_ref, beside_ref, slopes_ref, ahead_total, beside_total):
    own_products(((1, RUN - 1), True), block_rows(ahead_ref, beside_ref), beside_ref, slopes_ref, ahead_total, beside_total)


def pair(own_ref, other_ref, scalars_ref, total_in, loss_in, loss_ref, image_if_even, store, ids=None):
    scale, shift = scale_and_shift(scalars_ref)
    own_ref, other_ref = block_rows(own_ref, total_in), block_rows(other_ref, total_in)
    down = None if ids is None else ids_down(ids[0])
    chunks = halves(own_ref.shape[0])

    def scores(chunk):
        return scale * product(own_ref[chunk, :], other_ref[...], 1, 1) + shift

    def body(counted):
        logits = scores(chunks[0])
        for at, chunk in enumerate(chunks):
            positive = None if ids is None else match(down[chunk, :], ids[1])
            small = jnp.exp(-jnp.abs(logits))
            slopes = slopes_of(logits, small, positive)
            if counted:
                loss_ref[chunk, :] = loss_in[chunk, :] + fold(terms_of(logits, small, positive))
            else:
                loss_ref[chunk, :] = loss_in[chunk, :]
            if at + 1 < len(chunks):
                logits = scores(chunks[at + 1])
            store(chunk, total_in[chunk, :] + product(slopes, other_ref[...], 1, 0))

    by_parity(image_if_even, body)


def keep(total_ref):
    def store(chunk, total):
        total_ref[chunk, :] = total

    return store


def near_kernel(ahead_ref, own_ref, other_ref, own_slopes_ref, ids_ref, scalars_ref, ahead_in, total_in, loss_in, ahead_total, total_ref, loss_ref):
    own_products(((1, RUN - 1), False), block_rows(ahead_ref, own_ref), own_ref, own_slopes_ref, ahead_total, total_ref)
    ids = (ids_ref[...], read_ids(other_ref, own_ref.shape[0]))
    pair(own_ref, other_ref, scalars_ref, total_ref, loss_in, loss_ref, False, keep(total_ref), ids)


def far_kernel(image_if_even, where, own_ref, other_ref, scalars_ref, total_in, loss_in, total_ref, loss_ref):
    on_some(where, lambda: pair(own_ref, other_ref, scalars_ref, total_in, loss_in, loss_ref, image_if_even, keep(total_ref)))


def beside_kernel(own_ref, other_ref, scalars_ref, total_in, loss_in, rounded_ref, loss_ref):
    scale, _ = scale_and_shift(scalars_ref)

    def store(chunk, total):
        rounded_ref[chunk, :] = (scale * total).astype(jnp.bfloat16)

    pair(own_ref, other_ref, scalars_ref, total_in, loss_in, loss_ref, False, store)


def ahead_kernel(own_ref, other_ref, scalars_ref, total_in, loss_in, beside_ref, row_loss_ref, image_ref, text_ref, rounded_ref, losses_ref, sems):
    scale, shift = scale_and_shift(scalars_ref)
    own_ref, other_ref = block_rows(own_ref, total_in), block_rows(other_ref, total_in)
    rows = total_in.shape[0]
    chunks = halves(rows)

    def scores(chunk):
        return scale * product(own_ref[chunk, :], other_ref[...], 1, 1) + shift

    def body(even):
        ahead_out, beside_out = (image_ref, text_ref) if even else (text_ref, image_ref)
        copies = [pltpu.make_async_copy(beside_ref, beside_out, sems.at[0])]
        copies[0].start()
        logits = scores(chunks[0])
        for at, chunk in enumerate(chunks):
            last = at + 1 == len(chunks)
            small = jnp.exp(-jnp.abs(logits))
            slopes = slopes_of(logits, small)
            loss = loss_in[chunk, :]
            if even:
                loss = loss + fold(terms_of(logits, small))
            losses_ref[:, chunk] = jnp.sum(loss.T, axis=0, keepdims=True) / (STEPS * rows)
            if last:
                copies.append(pltpu.make_async_copy(losses_ref, row_loss_ref, sems.at[at + 2]))
                copies[-1].start()
            else:
                logits = scores(chunks[at + 1])
            total = total_in[chunk, :] + product(slopes, other_ref[...], 1, 0)
            rounded_ref[chunk, :] = (scale * total).astype(jnp.bfloat16)
            copies.append(pltpu.make_async_copy(rounded_ref.at[chunk, :], ahead_out.at[chunk, :], sems.at[at + 1]))
            copies[-1].start()
        for copy in copies:
            copy.wait()

    by_parity(True, body)


def call(kernel, out_shape, in_specs, out_specs, scratch=(), aliases=None):
    return pl.pallas_call(
        kernel,
        out_shape=out_shape,
        in_specs=in_specs,
        out_specs=out_specs,
        scratch_shapes=scratch,
        input_output_aliases=aliases or {},
        cost_estimate=pl.CostEstimate(flops=1, bytes_accessed=1, transcendentals=0),
        compiler_params=pltpu.CompilerParams(vmem_limit_bytes=VMEM_LIMIT),
    )


def near(array):
    return pltpu.with_memory_space_constraint(array, pltpu.VMEM)


def local(image, text, ids, log_scale, logit_bias):
    size = lax.axis_size(AXES)
    rows, width = image.shape
    in_vmem = pl.BlockSpec(memory_space=pltpu.VMEM)
    anywhere = pl.BlockSpec(memory_space=pl.ANY)
    total_shape = pltpu.VMEM((rows, width), jnp.float32)
    loss_shape = pltpu.VMEM((rows, LANES), jnp.float32)
    slopes_shape = pltpu.VMEM((rows, rows), jnp.bfloat16)
    block_shape = pltpu.VMEM((rows, width), jnp.bfloat16)
    grad_shape = jax.ShapeDtypeStruct((rows, width), jnp.bfloat16)
    in_hbm = lambda array: pltpu.with_memory_space_constraint(array, pltpu.HBM)

    ahead = call(
        ahead_place_kernel,
        pltpu.VMEM((rows + SPARE, width), jnp.bfloat16),
        [anywhere] * 2,
        in_vmem,
        [pltpu.SemaphoreType.DMA],
    )(in_hbm(image), in_hbm(text))
    cross1 = lax.ppermute(ahead, AXES, swap_across(size))

    ids = ids.reshape(1, rows)
    with_ids = call(
        beside_place_kernel,
        pltpu.VMEM((rows + SPARE, width), jnp.bfloat16),
        [anywhere] * 2 + [in_vmem],
        in_vmem,
        [pltpu.SemaphoreType.DMA],
    )(in_hbm(text), in_hbm(after(image, ahead)), ids)
    scalars = jnp.where(lax.broadcasted_iota(jnp.int32, (8, LANES), 0) == 0, jnp.exp(log_scale), logit_bias)
    chip1 = lax.ppermute(with_ids, AXES, swap_in_chip(size))

    beside, own_slopes, loss = call(
        own_kernel,
        (block_shape, slopes_shape, loss_shape),
        [in_vmem] * 4,
        (in_vmem,) * 3,
        [pltpu.SemaphoreType.DMA],
    )(near(ahead), near(with_ids), ids, scalars)
    ahead_total, beside_total = call(
        early_products_kernel,
        (total_shape, total_shape),
        [in_vmem] * 3,
        (in_vmem,) * 2,
    )(near(ahead), near(beside), near(own_slopes))
    cross2 = lax.ppermute(after(beside, ahead_total), AXES, two_along(size))
    own_slopes, loss = call(
        later_scores_kernel,
        (slopes_shape, loss_shape),
        [in_vmem] * 6,
        (in_vmem,) * 2,
        aliases={4: 0, 5: 1},
    )(near(ahead), near(beside), ids, scalars, near(own_slopes), near(loss))

    far_specs = [in_vmem] * 5

    def far(image_if_even, own, other, total, loss, where=None):
        return call(
            functools.partial(far_kernel, image_if_even, where), (total_shape, loss_shape), far_specs, (in_vmem, in_vmem), aliases={3: 0, 4: 1}
        )(near(own), near(other), scalars, near(total), near(loss))

    ahead_total, beside_total, loss = call(
        near_kernel,
        (total_shape, total_shape, loss_shape),
        [in_vmem] * 9,
        (in_vmem,) * 3,
        aliases={6: 0, 7: 1, 8: 2},
    )(near(ahead), near(beside), near(chip1), near(own_slopes), ids, scalars, near(ahead_total), near(beside_total), near(loss))

    cross1 = after(cross1, loss)
    ahead_total, loss = far(True, ahead, cross1, ahead_total, loss, ((1,), True))
    cross3 = lax.ppermute(after(cross1, loss), AXES, two_along(size))
    ahead_total, loss = far(True, ahead, cross1, ahead_total, loss, ((1,), False))
    chip2 = lax.ppermute(after(cross1, loss)[:rows], AXES, swap_in_chip(size))
    chip3 = lax.ppermute(after(cross2, loss), AXES, swap_in_chip(size))
    beside_total, loss = far(False, beside, chip2, beside_total, loss)
    ahead_total, loss = far(True, ahead, cross2, ahead_total, loss)
    beside_grad, loss = call(
        beside_kernel,
        (block_shape, loss_shape),
        far_specs,
        (in_vmem, in_vmem),
        aliases={4: 1},
    )(near(beside), near(chip3), scalars, near(beside_total), near(loss))

    row_loss, grad_image, grad_text = call(
        ahead_kernel,
        (jax.ShapeDtypeStruct((1, rows), jnp.float32), grad_shape, grad_shape),
        far_specs + [in_vmem],
        (anywhere, anywhere, anywhere),
        [pltpu.VMEM((rows, width), jnp.bfloat16), pltpu.VMEM((1, rows), jnp.float32), pltpu.SemaphoreType.DMA((4,))],
    )(near(ahead), near(cross3), scalars, near(ahead_total), near(loss), near(beside_grad))
    return row_loss.reshape(rows), grad_image, grad_text


def solution(mesh):
    in_specs = (P(AXES, None), P(AXES, None), P(AXES), P(), P())
    out_specs = (P(AXES), P(AXES, None), P(AXES, None))
    return jax.shard_map(local, mesh=mesh, in_specs=in_specs, out_specs=out_specs, check_vma=False)
```

```python
import functools

import jax
import jax.numpy as jnp
from jax import lax
from jax.experimental import pallas as pl
from jax.experimental.pallas import tpu as pltpu
from jax.sharding import PartitionSpec as P

STEPS = 4
DIGITS = 3
AXES = ("rows", "cols")
LANES = 128
RUN = 16
SPARE = 16
VMEM_LIMIT = 24 * 1024 * 1024


def swap_in_chip(size):
    return [(i, i ^ 1) for i in range(size)]


def swap_across(size):
    return [(i, (i + 1) % size if i % 2 else (i - 1) % size) for i in range(size)]


def over_run_end(pairs):
    over = [(source, target) for source, target in pairs if source // RUN != target // RUN]
    return over, [pair for pair in pairs if pair not in over]


def two_along(size):
    return [(i, (i - 2) % size if i % 2 else (i + 2) % size) for i in range(size)]


def after(array, *others):
    return lax.optimization_barrier((array,) + others)[0]


def is_even():
    return lax.rem(lax.axis_index("cols"), 2) == 0


def product(left, right, over_left, over_right):
    return lax.dot_general(
        left, right, (((over_left,), (over_right,)), ((), ())), preferred_element_type=jnp.float32
    )


def scale_and_shift(scalars_ref):
    return scalars_ref[0:1, 0:1], scalars_ref[1:2, 0:1]


def fold(terms):
    total = terms[:, :LANES]
    for at in range(LANES, terms.shape[1], LANES):
        total = total + terms[:, at : at + LANES]
    return total


def by_parity(true_if_even, body):
    even = is_even()

    @pl.when(even)
    def _():
        body(true_if_even)

    @pl.when(jnp.logical_not(even))
    def _():
        body(not true_if_even)


def slopes_of(logits, small, positive=None):
    slopes = jnp.where(logits >= 0, 1.0, small) / (1.0 + small)
    if positive is not None:
        slopes = slopes - jnp.where(positive, 1.0, 0.0)
    return slopes.astype(jnp.bfloat16)


def terms_of(logits, small, positive=None):
    terms = jnp.maximum(logits, 0.0) + jnp.log1p(small)
    if positive is not None:
        terms = terms - jnp.where(positive, logits, 0.0)
    return terms


def copy_by_parity(if_even, if_odd, out, sem):
    even = is_even()
    copies = [(even, pltpu.make_async_copy(if_even, out, sem)), (jnp.logical_not(even), pltpu.make_async_copy(if_odd, out, sem))]
    for here, copy in copies:
        pl.when(here)(copy.start)

    def wait():
        for here, copy in copies:
            pl.when(here)(copy.wait)

    return wait


def ahead_place_kernel(even_ref, odd_ref, out_ref, sem):
    rows, width = even_ref.shape
    wait = copy_by_parity(even_ref, odd_ref, out_ref.at[:rows, :], sem)
    out_ref[rows:, :] = jnp.zeros((SPARE, width), out_ref.dtype)
    wait()


def beside_place_kernel(even_ref, odd_ref, ids_ref, out_ref, sem):
    rows, width = even_ref.shape
    wait = copy_by_parity(even_ref, odd_ref, out_ref.at[:rows, :], sem)
    spare = jnp.zeros((SPARE, width), jnp.float32)
    at_row = lax.broadcasted_iota(jnp.int32, (SPARE, rows), 0)
    ids = jnp.broadcast_to(ids_ref[...], (SPARE, rows))
    digits = jnp.zeros((SPARE, rows), jnp.int32)
    for digit in range(DIGITS):
        digits = jnp.where(at_row == digit, lax.shift_right_logical(ids, 6 * digit) & 63, digits)
    spare = jnp.concatenate([digits.astype(jnp.float32), spare[:, rows:]], axis=1)
    out_ref[rows:, :] = spare.astype(out_ref.dtype)
    wait()


def read_ids(with_ids_ref, rows):
    spare = with_ids_ref[rows:, :][:, :rows].astype(jnp.float32)
    place = lax.broadcasted_iota(jnp.int32, (SPARE, rows), 0)
    weights = jnp.zeros((SPARE, rows), jnp.float32)
    for digit in range(DIGITS):
        weights = jnp.where(place == digit, float(64**digit), weights)
    return jnp.sum(spare * weights, axis=0, keepdims=True).astype(jnp.int32)


def ids_down(ids):
    return jnp.broadcast_to(ids, (LANES, ids.shape[1])).T


def match(down, ids):
    parts = [down == ids[:, at : at + LANES] for at in range(0, ids.shape[1], LANES)]
    return jnp.concatenate(parts, axis=1)


def halves(rows):
    return [slice(0, rows // 2), slice(rows // 2, rows)]


def block_rows(ref, like):
    return ref.at[: like.shape[0], :]


def on_some(where, body):
    if where is None:
        body()
        return
    places, among = where
    at = lax.rem(lax.axis_index("cols"), RUN)
    here = functools.reduce(jnp.logical_or, [at == place for place in places])
    pl.when(here if among else jnp.logical_not(here))(body)


def own_scores(where, ahead_ref, beside_ref, ids_ref, scalars_ref, slopes_ref, loss_ref):
    def body(even):
        scale, shift = scale_and_shift(scalars_ref)
        ids = ids_ref[...]
        down = ids_down(ids)
        image_ref, text_ref = (ahead_ref, beside_ref) if even else (beside_ref, ahead_ref)
        for chunk in halves(image_ref.shape[0]):
            logits = scale * product(image_ref[chunk, :], text_ref[...], 1, 1) + shift
            small, positive = jnp.exp(-jnp.abs(logits)), match(down[chunk, :], ids)
            slopes_ref[chunk, :] = slopes_of(logits, small, positive)
            loss_ref[chunk, :] = fold(terms_of(logits, small, positive))

    on_some(where, lambda: by_parity(True, body))


def own_products(where, ahead_ref, beside_ref, slopes_ref, ahead_total, beside_total):
    def body(even):
        image_ref, text_ref = (ahead_ref, beside_ref) if even else (beside_ref, ahead_ref)
        image_total, text_total = (ahead_total, beside_total) if even else (beside_total, ahead_total)
        image_total[...] = product(slopes_ref[...], text_ref[...], 1, 0)
        text_total[...] = product(slopes_ref[...], image_ref[...], 0, 0)

    on_some(where, lambda: by_parity(True, body))


def own_kernel(ahead_ref, with_ids_ref, ids_ref, scalars_ref, beside_ref, slopes_ref, loss_ref, sem):
    beside_copy = pltpu.make_async_copy(block_rows(with_ids_ref, beside_ref), beside_ref, sem)
    beside_copy.start()
    ahead_ref, with_ids_ref = block_rows(ahead_ref, beside_ref), block_rows(with_ids_ref, beside_ref)
    own_scores(((0,), False), ahead_ref, with_ids_ref, ids_ref, scalars_ref, slopes_ref, loss_ref)
    beside_copy.wait()


def later_scores_kernel(ahead_ref, beside_ref, ids_ref, scalars_ref, slopes_in, loss_in, slopes_ref, loss_ref):
    own_scores(((0,), True), block_rows(ahead_ref, beside_ref), beside_ref, ids_ref, scalars_ref, slopes_ref, loss_ref)


def early_products_kernel(ahead_ref, beside_ref, slopes_ref, ahead_total, beside_total):
    own_products(((1, RUN - 1), True), block_rows(ahead_ref, beside_ref), beside_ref, slopes_ref, ahead_total, beside_total)


def pair(own_ref, other_ref, scalars_ref, total_in, loss_in, loss_ref, image_if_even, store, ids=None):
    scale, shift = scale_and_shift(scalars_ref)
    own_ref, other_ref = block_rows(own_ref, total_in), block_rows(other_ref, total_in)
    down = None if ids is None else ids_down(ids[0])
    chunks = halves(own_ref.shape[0])

    def scores(chunk):
        return scale * product(own_ref[chunk, :], other_ref[...], 1, 1) + shift

    def body(counted):
        logits = scores(chunks[0])
        for at, chunk in enumerate(chunks):
            positive = None if ids is None else match(down[chunk, :], ids[1])
            small = jnp.exp(-jnp.abs(logits))
            slopes = slopes_of(logits, small, positive)
            if counted:
                loss_ref[chunk, :] = loss_in[chunk, :] + fold(terms_of(logits, small, positive))
            else:
                loss_ref[chunk, :] = loss_in[chunk, :]
            if at + 1 < len(chunks):
                logits = scores(chunks[at + 1])
            store(chunk, total_in[chunk, :] + product(slopes, other_ref[...], 1, 0))

    by_parity(image_if_even, body)


def keep(total_ref):
    def store(chunk, total):
        total_ref[chunk, :] = total

    return store


def near_kernel(ahead_ref, own_ref, other_ref, own_slopes_ref, ids_ref, scalars_ref, ahead_in, total_in, loss_in, ahead_total, total_ref, loss_ref):
    own_products(((1, RUN - 1), False), block_rows(ahead_ref, own_ref), own_ref, own_slopes_ref, ahead_total, total_ref)
    ids = (ids_ref[...], read_ids(other_ref, own_ref.shape[0]))
    pair(own_ref, other_ref, scalars_ref, total_ref, loss_in, loss_ref, False, keep(total_ref), ids)


def far_kernel(image_if_even, where, own_ref, other_ref, scalars_ref, total_in, loss_in, total_ref, loss_ref):
    on_some(where, lambda: pair(own_ref, other_ref, scalars_ref, total_in, loss_in, loss_ref, image_if_even, keep(total_ref)))


def beside_kernel(own_ref, other_ref, scalars_ref, total_in, loss_in, rounded_ref, loss_ref):
    scale, _ = scale_and_shift(scalars_ref)

    def store(chunk, total):
        rounded_ref[chunk, :] = (scale * total).astype(jnp.bfloat16)

    pair(own_ref, other_ref, scalars_ref, total_in, loss_in, loss_ref, False, store)


def ahead_kernel(where, own_ref, other_ref, scalars_ref, total_in, loss_in, beside_ref, row_loss_ref, image_ref, text_ref, rounded_ref, losses_ref, sems):
    scale, shift = scale_and_shift(scalars_ref)
    own_ref, other_ref = block_rows(own_ref, total_in), block_rows(other_ref, total_in)
    rows = total_in.shape[0]
    chunks = halves(rows)

    def scores(chunk):
        return scale * product(own_ref[chunk, :], other_ref[...], 1, 1) + shift

    def body(even):
        ahead_out, beside_out = (image_ref, text_ref) if even else (text_ref, image_ref)
        copies = [pltpu.make_async_copy(beside_ref, beside_out, sems.at[0])]
        copies[0].start()
        logits = scores(chunks[0])
        for at, chunk in enumerate(chunks):
            last = at + 1 == len(chunks)
            small = jnp.exp(-jnp.abs(logits))
            slopes = slopes_of(logits, small)
            loss = loss_in[chunk, :]
            if even:
                loss = loss + fold(terms_of(logits, small))
            losses_ref[:, chunk] = jnp.sum(loss.T, axis=0, keepdims=True) / (STEPS * rows)
            if last:
                copies.append(pltpu.make_async_copy(losses_ref, row_loss_ref, sems.at[at + 2]))
                copies[-1].start()
            else:
                logits = scores(chunks[at + 1])
            total = total_in[chunk, :] + product(slopes, other_ref[...], 1, 0)
            rounded_ref[chunk, :] = (scale * total).astype(jnp.bfloat16)
            copies.append(pltpu.make_async_copy(rounded_ref.at[chunk, :], ahead_out.at[chunk, :], sems.at[at + 1]))
            copies[-1].start()
        for copy in copies:
            copy.wait()

    on_some(where, lambda: by_parity(True, body))


def later_ahead_kernel(where, own_ref, other_ref, scalars_ref, total_in, loss_in, beside_ref, row_loss_in, image_in, text_in, *refs):
    del row_loss_in, image_in, text_in
    ahead_kernel(where, own_ref, other_ref, scalars_ref, total_in, loss_in, beside_ref, *refs)


def call(kernel, out_shape, in_specs, out_specs, scratch=(), aliases=None):
    return pl.pallas_call(
        kernel,
        out_shape=out_shape,
        in_specs=in_specs,
        out_specs=out_specs,
        scratch_shapes=scratch,
        input_output_aliases=aliases or {},
        cost_estimate=pl.CostEstimate(flops=1, bytes_accessed=1, transcendentals=0),
        compiler_params=pltpu.CompilerParams(vmem_limit_bytes=VMEM_LIMIT),
    )


def near(array):
    return pltpu.with_memory_space_constraint(array, pltpu.VMEM)


def local(image, text, ids, log_scale, logit_bias):
    size = lax.axis_size(AXES)
    rows, width = image.shape
    in_vmem = pl.BlockSpec(memory_space=pltpu.VMEM)
    anywhere = pl.BlockSpec(memory_space=pl.ANY)
    total_shape = pltpu.VMEM((rows, width), jnp.float32)
    loss_shape = pltpu.VMEM((rows, LANES), jnp.float32)
    slopes_shape = pltpu.VMEM((rows, rows), jnp.bfloat16)
    block_shape = pltpu.VMEM((rows, width), jnp.bfloat16)
    grad_shape = jax.ShapeDtypeStruct((rows, width), jnp.bfloat16)
    in_hbm = lambda array: pltpu.with_memory_space_constraint(array, pltpu.HBM)

    ahead = call(
        ahead_place_kernel,
        pltpu.VMEM((rows + SPARE, width), jnp.bfloat16),
        [anywhere] * 2,
        in_vmem,
        [pltpu.SemaphoreType.DMA],
    )(in_hbm(image), in_hbm(text))
    cross1 = lax.ppermute(ahead, AXES, swap_across(size))

    ids = ids.reshape(1, rows)
    with_ids = call(
        beside_place_kernel,
        pltpu.VMEM((rows + SPARE, width), jnp.bfloat16),
        [anywhere] * 2 + [in_vmem],
        in_vmem,
        [pltpu.SemaphoreType.DMA],
    )(in_hbm(text), in_hbm(after(image, ahead)), ids)
    scalars = jnp.where(lax.broadcasted_iota(jnp.int32, (8, LANES), 0) == 0, jnp.exp(log_scale), logit_bias)
    chip1 = lax.ppermute(with_ids, AXES, swap_in_chip(size))

    beside, own_slopes, loss = call(
        own_kernel,
        (block_shape, slopes_shape, loss_shape),
        [in_vmem] * 4,
        (in_vmem,) * 3,
        [pltpu.SemaphoreType.DMA],
    )(near(ahead), near(with_ids), ids, scalars)
    ahead_total, beside_total = call(
        early_products_kernel,
        (total_shape, total_shape),
        [in_vmem] * 3,
        (in_vmem,) * 2,
    )(near(ahead), near(beside), near(own_slopes))
    cross2 = lax.ppermute(after(beside, ahead_total), AXES, two_along(size))
    own_slopes, loss = call(
        later_scores_kernel,
        (slopes_shape, loss_shape),
        [in_vmem] * 6,
        (in_vmem,) * 2,
        aliases={4: 0, 5: 1},
    )(near(ahead), near(beside), ids, scalars, near(own_slopes), near(loss))

    far_specs = [in_vmem] * 5

    def far(image_if_even, own, other, total, loss, where=None):
        return call(
            functools.partial(far_kernel, image_if_even, where), (total_shape, loss_shape), far_specs, (in_vmem, in_vmem), aliases={3: 0, 4: 1}
        )(near(own), near(other), scalars, near(total), near(loss))

    ahead_total, beside_total, loss = call(
        near_kernel,
        (total_shape, total_shape, loss_shape),
        [in_vmem] * 9,
        (in_vmem,) * 3,
        aliases={6: 0, 7: 1, 8: 2},
    )(near(ahead), near(beside), near(chip1), near(own_slopes), ids, scalars, near(ahead_total), near(beside_total), near(loss))

    cross1 = after(cross1, loss)
    ahead_total, loss = far(True, ahead, cross1, ahead_total, loss, ((1,), True))
    over, inside = over_run_end(two_along(size))
    cross1_here = after(cross1, loss)
    cross3 = lax.ppermute(cross1_here, AXES, inside)
    cross3_over = lax.ppermute(cross1_here, AXES, over)
    ahead_total, loss = far(True, ahead, cross1, ahead_total, loss, ((1,), False))
    chip2 = lax.ppermute(after(cross1, loss)[:rows], AXES, swap_in_chip(size))
    chip3 = lax.ppermute(after(cross2, loss), AXES, swap_in_chip(size))
    beside_total, loss = far(False, beside, chip2, beside_total, loss)
    ahead_total, loss = far(True, ahead, cross2, ahead_total, loss)
    beside_grad, loss = call(
        beside_kernel,
        (block_shape, loss_shape),
        far_specs,
        (in_vmem, in_vmem),
        aliases={4: 1},
    )(near(beside), near(chip3), scalars, near(beside_total), near(loss))

    results = (jax.ShapeDtypeStruct((1, rows), jnp.float32), grad_shape, grad_shape)
    scratch = [pltpu.VMEM((rows, width), jnp.bfloat16), pltpu.VMEM((1, rows), jnp.float32), pltpu.SemaphoreType.DMA((4,))]
    operands = (scalars, near(ahead_total), near(loss), near(beside_grad))
    ends = (0, RUN - 1)
    results = call(
        functools.partial(ahead_kernel, (ends, False)), results, far_specs + [in_vmem], (anywhere,) * 3, scratch
    )(near(ahead), near(cross3), *operands)
    row_loss, grad_image, grad_text = call(
        functools.partial(later_ahead_kernel, (ends, True)),
        (jax.ShapeDtypeStruct((1, rows), jnp.float32), grad_shape, grad_shape),
        far_specs + [in_vmem] + [anywhere] * 3,
        (anywhere,) * 3,
        scratch,
        aliases={6: 0, 7: 1, 8: 2},
    )(near(ahead), near(cross3_over), *operands, *results)
    return row_loss.reshape(rows), grad_image, grad_text


def solution(mesh):
    in_specs = (P(AXES, None), P(AXES, None), P(AXES), P(), P())
    out_specs = (P(AXES), P(AXES, None), P(AXES, None))
    return jax.shard_map(local, mesh=mesh, in_specs=in_specs, out_specs=out_specs, check_vma=False)
```
